512 devices in a mesh: tgt: 8 (over x, y_lo), blk: 64 (over z, y_hi, core).
Axes of the slice: x: 4, y: 8 (y_hi: 4, y_lo: 2; y = y_hi * 2 + y_lo), z: 8, core: 2. Of those that a mesh axis runs over, the one named last changes fastest.
Arguments:
- queries: bfloat16 [65536, 1024], P(('tgt', 'blk')), may hold values from -184 to 184
- keys: bfloat16 [256, 1024], P('blk'), may hold values from -6.1 to 6.1
- values: bfloat16 [256, 1024], P('blk'), may hold values from -6 to 6
- out_grad: bfloat16 [65536, 1024], P(('tgt', 'blk')), may hold values from -24 to 24
Outputs:
- query_grad: bfloat16 [65536, 1024], P(('tgt', 'blk'))
- key_grad: bfloat16 [256, 1024], P('blk', 'tgt')
- value_grad: bfloat16 [256, 1024], P('blk', 'tgt')
The draws below stay inside these ranges and needn't reach their ends.
All inputs are finite; a program needn't handle non-finite values.
Results may differ from the reference program's by a relative error of at most 0.035.
Values may be sent and summed in bfloat16 or wider, within the bound.
No kernel may reach another device: no remote copies, remote signals or barrier semaphores. Data moves between devices by JAX's collectives and lax.ppermute only.
A program may use at most 64 MiB of HBM per device.

```python
import jax
import jax.numpy as jnp
from jax import lax

D = 1024
H = 16
HD = 64
S = 256
TQALL = 65536


def shared_keys(key):
    return jnp.clip(jax.random.normal(key, (S, D), jnp.float32), -6.0, 6.0)


def draw_keys(key, part):
    base = shared_keys(key)
    return base.astype(jnp.bfloat16)


def draw_queries(key, part):
    key = jax.random.fold_in(key, 7)
    drawn = jnp.clip(jax.random.normal(key, (TQALL, D), jnp.float32), -6.0, 6.0)
    return drawn.astype(jnp.bfloat16)


def raised(result, own_key, source, target, parts, factor):
    owner, partner = [(jnp.arange(result.shape[position]) // (result.shape[position] // parts)).reshape([-1 if axis == position else 1 for axis in range(result.ndim)]) for position in (source, target)]
    chosen = jax.random.permutation(own_key, parts)[partner]
    strong = (owner == chosen) | (owner == (partner + parts // 2) % parts)
    return jnp.where(strong, factor * result, result)


def block_levels(key, dims, shards, least, largest):
    factor_of, own = 1.0, jax.random.fold_in(key, 6)
    for axis_at, parts in shards:
        steps = jnp.exp(jax.random.uniform(jax.random.fold_in(own, axis_at), (parts,), jnp.float32, least / len(shards), largest / len(shards)))
        factor_of = factor_of * jnp.repeat(steps, dims[axis_at] // parts).reshape([-1 if axis == axis_at else 1 for axis in range(len(dims))])
    return factor_of


def gaussian(rng, shape, deviation, bound, cuts=(), held_as=jnp.bfloat16):
    level = block_levels(rng, shape, cuts, -0.22, 0.18) if cuts else 1.0
    drawn = jax.random.normal(rng, shape, jnp.float32) * deviation * level
    return jnp.minimum(jnp.maximum(drawn, -bound), bound).astype(held_as)


def noise_with(rng, shape, deviation, most, cuts, heavy, held_as=jnp.bfloat16):
    result = deviation * jax.random.normal(rng, shape, jnp.float32)
    if cuts:
        result = result * block_levels(rng, shape, cuts, -0.22, 0.18)
    return jnp.clip(raised(result, jax.random.fold_in(rng, 3), *heavy), -most, most).astype(held_as)


def setup_inputs(seed: int = 0) -> dict:
    seeds = jax.random.split(jax.random.key(seed), 5)
    return {
        "queries": draw_queries(jax.random.fold_in(seeds[4], 71), 0),
        "keys": draw_keys(jax.random.fold_in(seeds[4], 71), 0),
        "values": gaussian(seeds[2], (S, D), 1.0, 6.0, ((0, 64),)),
        "out_grad": noise_with(seeds[3], (TQALL, D), 1.0, 24.0, ((0, 512),), (0, 1, 512, 6.0)),
    }


def block_grads(q_rows, do_rows, keys, values):
    rows = q_rows.shape[0]
    scale = HD ** -0.5
    q = q_rows.astype(jnp.float32).reshape(rows, H, HD)
    dout = do_rows.astype(jnp.float32).reshape(rows, H, HD)
    k = keys.astype(jnp.float32).reshape(S, H, HD)
    v = values.astype(jnp.float32).reshape(S, H, HD)
    scores = jnp.einsum('rhd,shd->hrs', q, k) * scale
    top = jnp.max(scores, axis=-1, keepdims=True)
    expo = jnp.exp(scores - top)
    probs = expo / jnp.sum(expo, axis=-1, keepdims=True)
    probs_low = probs.astype(jnp.bfloat16).astype(jnp.float32)
    output = jnp.einsum('hrs,shd->rhd', probs_low, v)
    delta = jnp.transpose(jnp.sum(dout * output, axis=-1))
    dprob = jnp.einsum('rhd,shd->hrs', dout, v)
    dscore = probs * (dprob - delta[:, :, None])
    dscore_low = dscore.astype(jnp.bfloat16).astype(jnp.float32)
    dq = (jnp.einsum('hrs,shd->rhd', dscore_low, k) * scale).reshape(rows, D)
    dk = (jnp.einsum('hrs,rhd->shd', dscore_low, q) * scale).reshape(S, D)
    dv = jnp.einsum('hrs,rhd->shd', probs_low, dout).reshape(S, D)
    return dq.astype(jnp.bfloat16), dk, dv


def reference(queries, keys, values, out_grad):
    block_rows = min(2048, TQALL)
    count = TQALL // block_rows
    q_blocks = queries.reshape(count, block_rows, D)
    do_blocks = out_grad.reshape(count, block_rows, D)

    def step(carry, pair):
        dq, dk, dv = block_grads(pair[0], pair[1], keys, values)
        return (carry[0] + dk, carry[1] + dv), dq

    start = (jnp.zeros((S, D), jnp.float32), jnp.zeros((S, D), jnp.float32))
    (dk_sum, dv_sum), dq_blocks = lax.scan(step, start, (q_blocks, do_blocks))
    return dq_blocks.reshape(TQALL, D), dk_sum.astype(jnp.bfloat16), dv_sum.astype(jnp.bfloat16)
```

```python
import jax
import jax.numpy as jnp
from jax import lax
from jax.experimental import pallas as pl
from jax.experimental.pallas import tpu as pltpu
from jax.sharding import Mesh, PartitionSpec as P

HD = 64
PAIR = 2 * HD
SCALE = HD ** (-0.5)
LOG2E = 1.4426950408889634
BF16 = jnp.bfloat16
F32 = jnp.float32
OTHER = [(0, 1), (1, 0)]
SOURCE_AXES = ("z", "yhi")


def matmul(a, b):
    return lax.dot_general(a, b, (((1,), (0,)), ((), ())), preferred_element_type=F32)


def matmul_bt(a, b):
    return lax.dot_general(a, b, (((1,), (1,)), ((), ())), preferred_element_type=F32)


def split_heads(a, axis):
    first = lax.broadcasted_iota(jnp.int32, a.shape, 1) < HD
    zero = jnp.zeros_like(a)
    return jnp.concatenate([jnp.where(first, a, zero), jnp.where(first, zero, a)], axis=axis)


def attention_kernel(near_ref, far_ref, kv_ref, dq_near_ref, dq_far_ref, dkv_ref, p_ref, ds_ref):
    sources = kv_ref.shape[0]
    width = kv_ref.shape[1] // 2
    rows = near_ref.shape[2]
    blocks = [(near_ref, dq_near_ref, 0), (near_ref, dq_near_ref, 1), (far_ref, dq_far_ref, 0), (far_ref, dq_far_ref, 1)]
    for low in range(0, width, PAIR):
        cols = slice(low, low + PAIR)
        k = kv_ref[:, cols]
        k2 = split_heads(k, 0)
        v2 = split_heads(kv_ref[:, width + low : width + low + PAIR], 0)
        k2t = k2.T
        for at, (ref, dq_ref, part) in enumerate(blocks):
            span = slice(at * rows, (at + 1) * rows)
            score = matmul_bt(k2, ref[part, 0, :, cols]) * (SCALE * LOG2E)
            dprob = matmul_bt(v2, ref[part, 1, :, cols])
            score = score.reshape(2, sources, rows)
            dprob = dprob.reshape(2, sources, rows)
            expo = jnp.exp2(score - jnp.max(score, axis=1, keepdims=True))
            probs = expo * (1.0 / jnp.sum(expo, axis=1, keepdims=True))
            p_low = probs.astype(BF16)
            delta = jnp.sum(p_low.astype(F32) * dprob, axis=1, keepdims=True)
            ds_low = (probs * (dprob - delta)).astype(BF16)
            p_ref[:, :, span] = p_low
            ds_ref[:, :, span] = ds_low
            dq_t = matmul(k2t, ds_low.reshape(2 * sources, rows)) * SCALE
            dq_ref[part, :, cols] = dq_t.T.astype(BF16)
        q = jnp.concatenate([ref[part, 0, :, cols] for ref, _, part in blocks], axis=0)
        do = jnp.concatenate([ref[part, 1, :, cols] for ref, _, part in blocks], axis=0)
        dk = matmul(jnp.concatenate([ds_ref[0], ds_ref[1]], axis=1), split_heads(q, 0)) * SCALE
        dv = matmul(jnp.concatenate([p_ref[0], p_ref[1]], axis=1), split_heads(do, 0))
        dkv_ref[:, cols] = dk.astype(BF16)
        dkv_ref[:, width + low : width + low + PAIR] = dv.astype(BF16)


def attention(near, far, kv):
    _, _, rows, width = near.shape
    sources = kv.shape[0]
    vmem = pl.BlockSpec(memory_space=pltpu.VMEM)
    pairs = 2 * 2 * rows * sources * width // HD
    return pl.pallas_call(
        attention_kernel,
        out_shape=(
            jax.ShapeDtypeStruct((2, rows, width), BF16),
            jax.ShapeDtypeStruct((2, rows, width), BF16),
            jax.ShapeDtypeStruct((sources, 2 * width), BF16),
        ),
        in_specs=[vmem] * 3,
        out_specs=(vmem, vmem, vmem),
        scratch_shapes=[
            pltpu.VMEM((2, sources, 4 * rows), BF16),
            pltpu.VMEM((2, sources, 4 * rows), BF16),
        ],
        compiler_params=pltpu.CompilerParams(vmem_limit_bytes=32 * 1024 * 1024),
        cost_estimate=pl.CostEstimate(flops=20 * pairs * HD, bytes_accessed=2 * 1024 * 1024, transcendentals=pairs),
    )(near, far, kv)


def pick(flag, a, b):
    return jnp.where(flag, a, b)


def shards(queries, keys, values, out_grad):
    rows, model = queries.shape
    held = keys.shape[0]
    half = model // 2
    core = lax.axis_index("core") == 0
    side = lax.axis_index("ylo") == 0
    chips = lax.axis_size(SOURCE_AXES)
    xs = lax.axis_size("x")

    packed = jnp.concatenate([queries, out_grad, keys, values], axis=0)
    kept = pick(core, packed[:, :half], packed[:, half:])
    moved = lax.ppermute(pick(core, packed[:, half:], packed[:, :half]), "core", OTHER)

    def source_rows(low):
        a, b = kept[low : low + held], moved[low : low + held]
        both = pick(core, jnp.concatenate([a, b], axis=0), jnp.concatenate([b, a], axis=0))
        both = both.reshape(2 * held, half // (2 * PAIR), 2, PAIR)
        return pick(side, both[:, :, 0], both[:, :, 1]).reshape(2 * held, half // 2)

    block = jnp.concatenate([source_rows(2 * rows), source_rows(2 * rows + held)], axis=1)

    targets = jnp.stack([kept[: 2 * rows], moved[: 2 * rows]])
    targets = targets.reshape(2, 2, rows, half // (2 * PAIR), 2, PAIR)
    one, two = targets[:, :, :, :, 0], targets[:, :, :, :, 1]
    shape = (2, 2, rows, half // 2)
    near = pick(side, one, two).reshape(shape)
    far = lax.ppermute(pick(side, two, one).reshape(shape), "ylo", OTHER)

    kv = lax.all_to_all(jnp.broadcast_to(block, (chips,) + block.shape), SOURCE_AXES, 0, 0, tiled=True)
    dq_near, dq_far, dkv = attention(near, far, kv.reshape(chips * 2 * held, half))

    dq_back = lax.ppermute(dq_far, "ylo", OTHER)
    parts = (2, rows, half // (2 * PAIR), 1, PAIR)
    a, b = dq_near.reshape(parts), dq_back.reshape(parts)
    dq = jnp.concatenate([pick(side, a, b), pick(side, b, a)], axis=3).reshape(2, rows, half)
    dq_home = lax.ppermute(dq[1], "core", OTHER)
    query_grad = jnp.concatenate([pick(core, dq[0], dq_home), pick(core, dq_home, dq[0])], axis=1)

    parts = lax.all_to_all(dkv.reshape(chips, 2 * held, half), SOURCE_AXES, 0, 0, tiled=True)
    total = jnp.sum(parts.astype(F32), axis=0).reshape(2, held, 2, half // (2 * PAIR), PAIR)
    total = jnp.transpose(total, (3, 0, 1, 2, 4)).reshape(xs // 2, 2, held, 2 * PAIR)
    none = jnp.zeros_like(total)
    outgoing = jnp.concatenate([pick(core, total, none), pick(core, none, total)], axis=0)
    mine = lax.all_to_all(outgoing.reshape(2 * xs, held, 2 * PAIR), ("x", "core"), 0, 0, tiled=True)
    mine = jnp.sum(mine, axis=0)
    return query_grad, mine[:, :PAIR].astype(BF16), mine[:, PAIR:].astype(BF16)


def solution(mesh):
    fine = Mesh(mesh.devices.reshape(4, 2, 8, 4, 2), ("x", "ylo", "z", "yhi", "core"))
    targets = ("x", "ylo", "z", "yhi", "core")
    sources = ("z", "yhi", "core")
    return jax.shard_map(
        shards,
        mesh=fine,
        in_specs=(P(targets, None), P(sources, None), P(sources, None), P(targets, None)),
        out_specs=(P(targets, None), P(sources, ("x", "ylo")), P(sources, ("x", "ylo"))),
        check_vma=False,
    )
```

```python
import math

import jax
import jax.numpy as jnp
from jax import lax
from jax.experimental import pallas as pl
from jax.experimental.pallas import tpu as pltpu
from jax.sharding import Mesh, PartitionSpec as P

HD = 64
PAIR = 2 * HD
TAIL = 16
HELD = 4
WIDE = 8
SCALE = HD ** (-0.5)
LOG2E = 1.4426950408889634
BF16 = jnp.bfloat16
F32 = jnp.float32
HEAD_AXES = ("x", "ylo", "core")
SOURCE_AXES = ("z", "yhi")


def matmul(a, b):
    return lax.dot_general(a, b, (((1,), (0,)), ((), ())), preferred_element_type=F32)


def matmul_bt(a, b):
    return lax.dot_general(a, b, (((1,), (1,)), ((), ())), preferred_element_type=F32)


def split_lanes(a):
    first = lax.broadcasted_iota(jnp.int32, a.shape, 1) < HD
    zero = jnp.zeros_like(a)
    return jnp.concatenate([jnp.where(first, a, zero), jnp.where(first, zero, a)], axis=0)


def join(a, b, part):
    cols = slice(part * HD, (part + 1) * HD)
    return jnp.concatenate([a[:, cols], b[:, cols]], axis=1)


def pack_kernel(all_ref, out_ref):
    rows = out_ref.shape[1] - TAIL
    model = all_ref.shape[1]
    held = HELD
    zero = jnp.zeros((TAIL - held, PAIR), F32)
    for low in range(0, model, PAIR):
        cols = slice(low, low + PAIR)
        q, do = all_ref[:rows, cols], all_ref[rows : 2 * rows, cols]
        kv = all_ref[2 * rows :, cols].astype(F32)
        k, v = kv[:held], kv[held : 2 * held]
        for part in range(2):
            head = low // HD + part
            out_ref[head, :rows, :] = join(q, do, part)
            tail = jnp.concatenate([join(k, v, part), zero], axis=0)
            out_ref[head, rows:, :] = tail.astype(BF16)


def attention_kernel(x_ref, kv_ref, dq_ref, dkv_ref):
    sources = kv_ref.shape[0]
    blocks, rows = x_ref.shape[0], x_ref.shape[1] - TAIL
    kv = kv_ref[...]
    kv2 = split_lanes(kv)
    kt = kv.T[:HD]
    total = None
    for b in range(0, blocks, WIDE):
        x = jnp.concatenate([x_ref[b + i, :rows, :] for i in range(WIDE)], axis=0)
        both = matmul_bt(kv2, x)
        score = both[:sources] * (SCALE * LOG2E)
        dprob = both[sources:]
        expo = jnp.exp2(score - jnp.max(score, axis=0, keepdims=True))
        probs = expo * (1.0 / jnp.sum(expo, axis=0, keepdims=True))
        p_low = probs.astype(BF16)
        delta = jnp.sum(p_low.astype(F32) * dprob, axis=0, keepdims=True)
        ds_low = (probs * (dprob - delta)).astype(BF16)
        dq = (matmul(kt, ds_low) * SCALE).astype(BF16)
        for i in range(WIDE):
            dq_ref[b + i] = dq[:, i * rows : (i + 1) * rows]
        part = matmul(jnp.concatenate([ds_low, p_low], axis=1), split_lanes(x))
        total = part if total is None else total + part
    first = lax.broadcasted_iota(jnp.int32, total.shape, 1) < HD
    dkv_ref[...] = jnp.where(first, total * SCALE, total).astype(BF16)


def merge_kernel(dq_ref, parts_ref, out_ref):
    feats = dq_ref.shape[1]
    total = jnp.sum(parts_ref[...].astype(F32), axis=0)
    tail = jnp.concatenate([total, total], axis=0).astype(BF16)
    for b in range(dq_ref.shape[0]):
        out_ref[b, :feats, :] = dq_ref[b]
        out_ref[b, feats:, :] = tail


def finish_kernel(x_ref, dq_ref, dk_ref, dv_ref):
    heads = x_ref.shape[0]
    held = dk_ref.shape[0]
    for low in range(0, heads, 2):
        pair = jnp.concatenate([x_ref[low, :HD, :], x_ref[low + 1, :HD, :]], axis=0)
        dq_ref[:, low * HD : (low + 2) * HD] = pair.T
    group = lax.axis_index(("x", "ylo"))
    one = x_ref[2 * group, HD:, :].astype(F32)
    two = x_ref[2 * group + 1, HD:, :].astype(F32)
    lower = lax.axis_index("core") == 0
    one = jnp.where(lower, one[:held], one[held : 2 * held])
    two = jnp.where(lower, two[:held], two[held : 2 * held])
    dk_ref[...] = join(one, two, 0).astype(BF16)
    dv_ref[...] = join(one, two, 1).astype(BF16)


def call(kernel, out, *args, flops=0, transcendentals=0):
    vmem = pl.BlockSpec(memory_space=pltpu.VMEM)
    size = sum(a.size * a.dtype.itemsize for a in args) + sum(2 * math.prod(s) for s in out)
    return pl.pallas_call(
        kernel,
        out_shape=tuple(jax.ShapeDtypeStruct(s, BF16) for s in out),
        in_specs=[vmem] * len(args),
        out_specs=(vmem,) * len(out),
        compiler_params=pltpu.CompilerParams(vmem_limit_bytes=32 * 1024 * 1024),
        cost_estimate=pl.CostEstimate(flops=flops, bytes_accessed=size, transcendentals=transcendentals),
    )(*args)


def shards(queries, keys, values, out_grad):
    rows, model = queries.shape
    held = keys.shape[0]
    heads = model // HD
    chips = lax.axis_size(SOURCE_AXES)
    sources = 2 * held * chips

    none = jnp.zeros((TAIL - 2 * held, model), BF16)
    inputs = jnp.concatenate([queries, out_grad, keys, values, none], axis=0)
    (packed,) = call(pack_kernel, [(heads, rows + TAIL, PAIR)], inputs)
    packed = lax.all_to_all(packed, HEAD_AXES, 0, 0, tiled=True)
    block = jnp.concatenate([packed[0, rows : rows + held], packed[1, rows : rows + held]], axis=0)
    kv = lax.all_to_all(jnp.broadcast_to(block, (chips, 2 * held, PAIR)), SOURCE_AXES, 0, 0, tiled=True)

    pairs = heads * rows * sources
    dq, dkv = call(
        attention_kernel,
        [(heads, HD, rows), (sources, PAIR)],
        packed,
        kv.reshape(sources, PAIR),
        flops=16 * HD * pairs,
        transcendentals=pairs,
    )
    parts = lax.all_to_all(dkv.reshape(chips, 2 * held, PAIR), SOURCE_AXES, 0, 0, tiled=True)
    (merged,) = call(merge_kernel, [(heads, HD + TAIL, rows)], dq, parts)
    merged = lax.all_to_all(merged, HEAD_AXES, 0, 0, tiled=True)
    return call(finish_kernel, [(rows, model), (held, PAIR), (held, PAIR)], merged)


def solution(mesh):
    fine = Mesh(mesh.devices.reshape(4, 2, 8, 4, 2), ("x", "ylo", "z", "yhi", "core"))
    targets = ("x", "ylo", "z", "yhi", "core")
    sources = ("z", "yhi", "core")
    return jax.shard_map(
        shards,
        mesh=fine,
        in_specs=(P(targets, None), P(sources, None), P(sources, None), P(targets, None)),
        out_specs=(P(targets, None), P(sources, ("x", "ylo")), P(sources, ("x", "ylo"))),
        check_vma=False,
    )
```

```python
import math

import jax
import jax.numpy as jnp
from jax import lax
from jax.experimental import pallas as pl
from jax.experimental.pallas import tpu as pltpu
from jax.sharding import Mesh, PartitionSpec as P

HD = 64
PAIR = 2 * HD
SCALE = HD ** (-0.5)
LOG2E = 1.4426950408889634
BF16 = jnp.bfloat16
F32 = jnp.float32
SOURCE_AXES = ("z", "yhi")
CORE_SWAP = [(0, 1), (1, 0)]
BOTH_SWAP = [(0, 3), (1, 2), (2, 1), (3, 0)]


def matmul(a, b):
    return lax.dot_general(a, b, (((1,), (0,)), ((), ())), preferred_element_type=F32)


def matmul_bt(a, b):
    return lax.dot_general(a, b, (((1,), (1,)), ((), ())), preferred_element_type=F32)


def split_lanes(a):
    first = lax.broadcasted_iota(jnp.int32, a.shape, 1) < HD
    zero = jnp.zeros_like(a)
    return jnp.concatenate([jnp.where(first, a, zero), jnp.where(first, zero, a)], axis=0)


def columns(core, side, pair):
    return pl.ds(pl.multiple_of((4 * core + 2 * pair + side) * PAIR, PAIR), PAIR)


def spread_kernel(k_ref, v_ref, out_ref):
    side = lax.axis_index("ylo")
    for core in range(2):
        parts = [ref[:, columns(core, side, pair)] for ref in (k_ref, v_ref) for pair in range(2)]
        block = jnp.concatenate(parts, axis=1)
        for chip in range(out_ref.shape[0] // 2):
            out_ref[2 * chip + core] = block


def quarter_kernel(q_ref, do_ref, *out_refs):
    core, side = lax.axis_index("core"), lax.axis_index("ylo")
    for at, out_ref in enumerate(out_refs):
        for pair in range(2):
            cols = columns(core ^ (at & 1), side ^ (at >> 1), pair)
            low = slice(pair * PAIR, (pair + 1) * PAIR)
            out_ref[0, :, low] = q_ref[:, cols]
            out_ref[1, :, low] = do_ref[:, cols]


def attention_kernel(*refs):
    in_refs, kv_ref, dq_refs, dkv_ref, flat_ref = refs[:4], refs[4], refs[5:9], refs[9], refs[10]
    held = kv_ref.shape[1]
    for at in range(kv_ref.shape[0]):
        flat_ref[at * held : (at + 1) * held, :] = kv_ref[at].astype(F32)
    sources, width = flat_ref.shape[0], flat_ref.shape[1] // 2
    rows = in_refs[0].shape[1]
    for low in range(0, width, PAIR):
        cols = slice(low, low + PAIR)
        k2 = split_lanes(flat_ref[:, cols].astype(BF16))
        v2 = split_lanes(flat_ref[:, width + low : width + low + PAIR].astype(BF16))
        q = jnp.concatenate([ref[0, :, cols] for ref in in_refs], axis=0)
        do = jnp.concatenate([ref[1, :, cols] for ref in in_refs], axis=0)
        score = (matmul_bt(k2, q) * (SCALE * LOG2E)).reshape(2, sources, 4 * rows)
        dprob = matmul_bt(v2, do).reshape(2, sources, 4 * rows)
        expo = jnp.exp2(score - jnp.max(score, axis=1, keepdims=True))
        probs = expo * (1.0 / jnp.sum(expo, axis=1, keepdims=True))
        p_low = probs.astype(BF16)
        delta = jnp.sum(p_low.astype(F32) * dprob, axis=1, keepdims=True)
        ds_low = (probs * (dprob - delta)).astype(BF16)
        dk = matmul(jnp.concatenate([ds_low[0], ds_low[1]], axis=1), split_lanes(q)) * SCALE
        dv = matmul(jnp.concatenate([p_low[0], p_low[1]], axis=1), split_lanes(do))
        dkv_ref[:, cols] = dk.astype(BF16)
        dkv_ref[:, width + low : width + low + PAIR] = dv.astype(BF16)
        dq_t = (matmul(k2.T, ds_low.reshape(2 * sources, 4 * rows)) * SCALE).astype(BF16)
        for at, dq_ref in enumerate(dq_refs):
            dq_ref[:, cols] = dq_t[:, at * rows : (at + 1) * rows].T


def reduce_kernel(parts_ref, out_ref):
    total = jnp.sum(parts_ref[...].astype(F32), axis=0)
    held, width = out_ref.shape[1], total.shape[1] // 2
    core = lax.axis_index("core")
    for dest in range(out_ref.shape[0]):
        x, half = dest // 2, dest % 2
        low = (x % 2) * PAIR
        rows = total[half * held : (half + 1) * held]
        piece = jnp.concatenate([rows[:, low : low + PAIR], rows[:, width + low : width + low + PAIR]], axis=1)
        out_ref[dest] = jnp.where(core == x // 2, piece, jnp.zeros_like(piece))


def finish_kernel(own_ref, core_ref, side_ref, both_ref, mine_ref, dq_ref, dk_ref, dv_ref):
    core, side = lax.axis_index("core"), lax.axis_index("ylo")
    for at, ref in enumerate((own_ref, core_ref, side_ref, both_ref)):
        for pair in range(2):
            dq_ref[:, columns(core ^ (at & 1), side ^ (at >> 1), pair)] = ref[:, pair * PAIR : (pair + 1) * PAIR]
    total = jnp.sum(mine_ref[...], axis=0)
    dk_ref[...] = total[:, :PAIR].astype(BF16)
    dv_ref[...] = total[:, PAIR:].astype(BF16)


def call(kernel, out, *args, dtype=BF16, scratch=(), flops=0, transcendentals=0):
    vmem = pl.BlockSpec(memory_space=pltpu.VMEM)
    size = sum(a.size * a.dtype.itemsize for a in args) + sum(2 * math.prod(s) for s in out)
    return pl.pallas_call(
        kernel,
        out_shape=tuple(jax.ShapeDtypeStruct(s, dtype) for s in out),
        in_specs=[vmem] * len(args),
        out_specs=(vmem,) * len(out),
        scratch_shapes=scratch,
        compiler_params=pltpu.CompilerParams(vmem_limit_bytes=32 * 1024 * 1024),
        cost_estimate=pl.CostEstimate(flops=flops, bytes_accessed=size, transcendentals=transcendentals),
    )(*args)


def trade(arrays):
    own, core, side, both = arrays
    core = lax.ppermute(core, "core", CORE_SWAP)
    side = lax.ppermute(side, "ylo", CORE_SWAP)
    both = lax.ppermute(both, ("ylo", "core"), BOTH_SWAP)
    return own, core, side, both


def shards(queries, keys, values, out_grad):
    rows, model = queries.shape
    held = keys.shape[0]
    width = model // 4
    chips = lax.axis_size(SOURCE_AXES)
    sources = 2 * held * chips

    (spread,) = call(spread_kernel, [(2 * chips, held, 2 * width)], keys, values)
    kv = lax.all_to_all(spread, SOURCE_AXES + ("core",), 0, 0, tiled=True)
    targets = trade(call(quarter_kernel, [(2, rows, width)] * 4, queries, out_grad))

    pairs = 4 * rows * sources * width // HD
    *dq, dkv = call(
        attention_kernel,
        [(rows, width)] * 4 + [(sources, 2 * width)],
        *targets,
        kv,
        scratch=[pltpu.VMEM((sources, 2 * width), F32)],
        flops=20 * HD * pairs,
        transcendentals=pairs,
    )
    parts = lax.all_to_all(dkv.reshape(chips, 2 * held, 2 * width), SOURCE_AXES, 0, 0, tiled=True)
    dq = trade(dq)
    (outgoing,) = call(reduce_kernel, [(8, held, 2 * PAIR)], parts, dtype=F32)
    mine = lax.all_to_all(outgoing, ("x", "core"), 0, 0, tiled=True)
    return call(finish_kernel, [(rows, model), (held, PAIR), (held, PAIR)], *dq, mine)


def solution(mesh):
    fine = Mesh(mesh.devices.reshape(4, 2, 8, 4, 2), ("x", "ylo", "z", "yhi", "core"))
    targets = ("x", "ylo", "z", "yhi", "core")
    sources = ("z", "yhi", "core")
    return jax.shard_map(
        shards,
        mesh=fine,
        in_specs=(P(targets, None), P(sources, None), P(sources, None), P(targets, None)),
        out_specs=(P(targets, None), P(sources, ("x", "ylo")), P(sources, ("x", "ylo"))),
        check_vma=False,
    )
```

```python
import functools
import itertools
import math

import jax
import jax.numpy as jnp
from jax import lax
from jax.experimental import pallas as pl
from jax.experimental.pallas import tpu as pltpu
from jax.sharding import Mesh, PartitionSpec as P

HD = 64
PAIR = 2 * HD
SCALE = HD ** (-0.5)
LOG2E = 1.4426950408889634
BF16 = jnp.bfloat16
F32 = jnp.float32
AXES = ("xh", "xl", "ylo", "z", "yhi", "core")
SOURCE_AXES = ("z", "yhi", "core")
GRAD_AXES = ("xh", "ylo", "z", "yhi", "core")
SOURCE_FIRST = (7, 2, 0)
GRAD_FIRST = (0, 0, 4, 0, 0)
CORE_SWAP = [(0, 1), (1, 0)]
BOTH_SWAP = [(0, 3), (1, 2), (2, 1), (3, 0)]


def matmul(a, b):
    return lax.dot_general(a, b, (((1,), (0,)), ((), ())), preferred_element_type=F32)


def matmul_bt(a, b):
    return lax.dot_general(a, b, (((1,), (1,)), ((), ())), preferred_element_type=F32)


def split_lanes(a):
    first = lax.broadcasted_iota(jnp.int32, a.shape, 1) < HD
    zero = jnp.zeros_like(a)
    return jnp.concatenate([jnp.where(first, a, zero), jnp.where(first, zero, a)], axis=0)


def join(a, b, part):
    cols = slice(part * HD, (part + 1) * HD)
    return jnp.concatenate([a[:, cols], b[:, cols]], axis=1)


def columns(side, pair, x):
    return pl.ds(pl.multiple_of((4 * pair + 2 * side + x) * PAIR, PAIR), PAIR)


def core_columns(ref, side, pair):
    a, b = (ref[:, columns(side, pair, x)].astype(F32) for x in range(2))
    return join(a, b, 0).astype(ref.dtype), join(a, b, 1).astype(ref.dtype)


def spread_kernel(kv_ref, out_ref):
    side = lax.axis_index("xl")
    held = out_ref.shape[1]
    pieces = []
    for pair in range(2):
        a, b = (kv_ref[:, columns(side, pair, x)].astype(F32) for x in range(2))
        pieces.append([join(a, b, core) for core in range(2)])
    for core in range(2):
        parts = [piece[core][low : low + held] for low in (0, held) for piece in pieces]
        block = jnp.concatenate(parts, axis=1).astype(BF16)
        for chip in range(out_ref.shape[0] // 2):
            out_ref[2 * chip + core] = block


def quarter_kernel(q_ref, do_ref, *out_refs):
    lower, side = lax.axis_index("core") == 0, lax.axis_index("xl")
    for flip in range(2):
        for pair in range(2):
            low = slice(pair * PAIR, (pair + 1) * PAIR)
            for at, ref in enumerate((q_ref, do_ref)):
                one, two = core_columns(ref, side ^ flip, pair)
                out_refs[flip][at, :, low] = jnp.where(lower, one, two)
                out_refs[3 - flip][at, :, low] = jnp.where(lower, two, one)


def attention_kernel(source_order, grad_order, *refs):
    in_refs, kv_ref, dq_refs, dkv_hbm, flat_ref, dkv_ref, sems = refs[:4], refs[4], refs[5:9], *refs[9:]
    held = kv_ref.shape[1]
    for at, block in enumerate(source_order):
        flat_ref[block * held : (block + 1) * held, :] = kv_ref[at].astype(F32)
    sources, width = flat_ref.shape[0], flat_ref.shape[1] // 2
    blocks = sources // held
    places = {member: at for at, member in enumerate(grad_order)}
    rows = in_refs[0].shape[1]
    copies = []
    for low in range(0, width, PAIR):
        cols = slice(low, low + PAIR)
        k2 = split_lanes(flat_ref[:, cols].astype(BF16))
        v2 = split_lanes(flat_ref[:, width + low : width + low + PAIR].astype(BF16))
        q = jnp.concatenate([ref[0, :, cols] for ref in in_refs], axis=0)
        do = jnp.concatenate([ref[1, :, cols] for ref in in_refs], axis=0)
        score = (matmul_bt(k2, q) * (SCALE * LOG2E)).reshape(2, sources, 4 * rows)
        dprob = matmul_bt(v2, do).reshape(2, sources, 4 * rows)
        expo = jnp.exp2(score - jnp.max(score, axis=1, keepdims=True))
        probs = expo * (1.0 / jnp.sum(expo, axis=1, keepdims=True))
        p_low = probs.astype(BF16)
        delta = jnp.sum(p_low.astype(F32) * dprob, axis=1, keepdims=True)
        ds_low = (probs * (dprob - delta)).astype(BF16)
        dk = matmul(jnp.concatenate([ds_low[0], ds_low[1]], axis=1), split_lanes(q)) * SCALE
        dv = matmul(jnp.concatenate([p_low[0], p_low[1]], axis=1), split_lanes(do))
        for part in range(2):
            both = join(dk, dv, part)
            first = (low // HD + part) * blocks
            for at in range(blocks):
                dkv_ref[places[first + at]] = both[at * held : (at + 1) * held].astype(BF16)
            span = pl.ds(places[first] // blocks * blocks, blocks)
            copy = pltpu.make_async_copy(dkv_ref.at[span], dkv_hbm.at[span], sems.at[low // HD + part])
            copy.start()
            copies.append(copy)
        dq_t = (matmul(k2.T, ds_low.reshape(2 * sources, 4 * rows)) * SCALE).astype(BF16)
        for at, dq_ref in enumerate(dq_refs):
            dq_ref[:, cols] = dq_t[:, at * rows : (at + 1) * rows].T
    for copy in copies:
        copy.wait()


def assemble_kernel(own_ref, side_ref, both_ref, core_ref, dq_ref):
    lower, side = lax.axis_index("core") == 0, lax.axis_index("xl")
    for flip, (near_ref, far_ref) in enumerate(((own_ref, core_ref), (side_ref, both_ref))):
        for pair in range(2):
            low = slice(pair * PAIR, (pair + 1) * PAIR)
            near, far = near_ref[:, low].astype(F32), far_ref[:, low].astype(F32)
            one, two = jnp.where(lower, near, far), jnp.where(lower, far, near)
            for x in range(2):
                dq_ref[:, columns(side ^ flip, pair, x)] = join(one, two, x).astype(BF16)


def total_kernel(parts_ref, dk_ref, dv_ref):
    one, two = (sum_parts(parts_ref, core) for core in range(2))
    dk_ref[...] = join(one, two, 0).astype(BF16)
    dv_ref[...] = join(one, two, 1).astype(BF16)


def sum_parts(parts_ref, core):
    terms = [parts_ref[at].astype(F32) for at in range(core, parts_ref.shape[0], 2)]
    while len(terms) > 1:
        terms = [a + b for a, b in zip(terms[::2], terms[1::2])]
    return terms[0]


def call(kernel, out, *args, last=pltpu.VMEM, scratch=(), flops=0, transcendentals=0):
    vmem = pl.BlockSpec(memory_space=pltpu.VMEM)
    size = sum(a.size * a.dtype.itemsize for a in args) + sum(2 * math.prod(s) for s in out)
    return pl.pallas_call(
        kernel,
        out_shape=tuple(jax.ShapeDtypeStruct(s, BF16) for s in out),
        in_specs=[vmem] * len(args),
        out_specs=(vmem,) * (len(out) - 1) + (pl.BlockSpec(memory_space=last),),
        scratch_shapes=scratch,
        compiler_params=pltpu.CompilerParams(vmem_limit_bytes=32 * 1024 * 1024),
        cost_estimate=pl.CostEstimate(flops=flops, bytes_accessed=size, transcendentals=transcendentals),
    )(*args)


def members(axes, first):
    sizes = [lax.axis_size(axis) for axis in axes]
    order = []
    for place in itertools.product(*map(range, sizes)):
        index = 0
        for at, start, size in zip(place, first, sizes):
            index = index * size + (at + start) % size
        order.append(index)
    return order


def trade(own, side, both, core):
    side = lax.ppermute(side, "xl", CORE_SWAP)
    both = lax.ppermute(both, ("xl", "core"), BOTH_SWAP)
    core = lax.ppermute(core, "core", CORE_SWAP)
    return own, side, both, core


def shards(queries, keys, values, out_grad):
    rows, model = queries.shape
    held = keys.shape[0]
    width = model // 4
    source_order = members(SOURCE_AXES, SOURCE_FIRST)
    grad_order = members(GRAD_AXES, GRAD_FIRST)
    blocks = len(source_order)
    sources = held * blocks

    (spread,) = call(spread_kernel, [(blocks, held, 2 * width)], jnp.concatenate([keys, values], axis=0))
    kv = lax.all_to_all(spread, SOURCE_AXES, 0, 0, axis_index_groups=[source_order], tiled=True)
    targets = trade(*call(quarter_kernel, [(2, rows, width)] * 4, queries, out_grad))

    pairs = 4 * rows * sources * width // HD
    *dq, dkv = call(
        functools.partial(attention_kernel, source_order, grad_order),
        [(rows, width)] * 4 + [(len(grad_order), held, PAIR)],
        *targets,
        kv,
        last=pl.ANY,
        scratch=[
            pltpu.VMEM((sources, 2 * width), F32),
            pltpu.VMEM((len(grad_order), held, PAIR), BF16),
            pltpu.SemaphoreType.DMA((width // HD,)),
        ],
        flops=20 * HD * pairs,
        transcendentals=pairs,
    )
    parts = lax.all_to_all(dkv, GRAD_AXES, 0, 0, axis_index_groups=[grad_order], tiled=True)
    (query_grad,) = call(assemble_kernel, [(rows, model)], *trade(*dq))
    key_grad, value_grad = call(total_kernel, [(held, PAIR), (held, PAIR)], parts)
    return query_grad, key_grad, value_grad


def solution(mesh):
    fine = Mesh(mesh.devices.reshape(2, 2, 2, 8, 4, 2), AXES)
    return jax.shard_map(
        shards,
        mesh=fine,
        in_specs=(P(AXES, None), P(AXES[3:], None), P(AXES[3:], None), P(AXES, None)),
        out_specs=(P(AXES, None), P(AXES[3:], AXES[:3]), P(AXES[3:], AXES[:3])),
        check_vma=False,
    )
```

```python
import functools
import itertools
import math

import jax
import jax.numpy as jnp
import numpy as np
from jax import lax
from jax.experimental import pallas as pl
from jax.experimental.pallas import tpu as pltpu
from jax.sharding import Mesh, PartitionSpec as P

HD = 64
PAIR = 2 * HD
SCALE = HD ** (-0.5)
LOG2E = 1.4426950408889634
BF16 = jnp.bfloat16
F32 = jnp.float32
AXES = ("xh", "xl", "ylo", "z", "yhi", "core")
SOURCE_AXES = ("z", "yhi", "core")
GRAD_AXES = ("xh", "ylo", "z", "yhi", "core")
SOURCE_ORDER = ((7, 0, 1, 2, 3, 4, 5, 6), (2, 3, 0, 1), (0, 1))
GRAD_ORDER = ((1, 0), (0, 1), (5, 6, 7, 0, 1, 2, 3, 4), (0, 1, 2, 3), (0, 1))
CORE_SWAP = [(0, 1), (1, 0)]
BOTH_SWAP = [(0, 3), (1, 2), (2, 1), (3, 0)]


def matmul(a, b):
    return lax.dot_general(a, b, (((1,), (0,)), ((), ())), preferred_element_type=F32)


def matmul_bt(a, b):
    return lax.dot_general(a, b, (((1,), (1,)), ((), ())), preferred_element_type=F32)


def split_lanes(a):
    first = lax.broadcasted_iota(jnp.int32, a.shape, 1) < HD
    zero = jnp.zeros_like(a)
    return jnp.concatenate([jnp.where(first, a, zero), jnp.where(first, zero, a)], axis=0)


def join(a, b, part):
    cols = slice(part * HD, (part + 1) * HD)
    return jnp.concatenate([a[:, cols], b[:, cols]], axis=1)


def columns(side, pair, x):
    return pl.ds(pl.multiple_of((4 * pair + 2 * side + x) * PAIR, PAIR), PAIR)


def core_columns(ref, side, pair):
    a, b = (ref[:, columns(side, pair, x)].astype(F32) for x in range(2))
    return join(a, b, 0).astype(ref.dtype), join(a, b, 1).astype(ref.dtype)


def spread_kernel(order, kv_ref, out_ref):
    side = lax.axis_index("xl")
    held = out_ref.shape[1]
    pieces = []
    for pair in range(2):
        a, b = (kv_ref[:, columns(side, pair, x)].astype(F32) for x in range(2))
        pieces.append([join(a, b, core) for core in range(2)])
    for core in range(2):
        parts = [piece[core][low : low + held] for low in (0, held) for piece in pieces]
        block = jnp.concatenate(parts, axis=1).astype(BF16)
        for at, member in enumerate(order):
            if member % 2 == core:
                out_ref[at] = block


def quarter_kernel(q_ref, do_ref, *out_refs):
    lower, side = lax.axis_index("core") == 0, lax.axis_index("xl")
    for flip in range(2):
        for pair in range(2):
            low = slice(pair * PAIR, (pair + 1) * PAIR)
            for at, ref in enumerate((q_ref, do_ref)):
                one, two = core_columns(ref, side ^ flip, pair)
                out_refs[flip][at, :, low] = jnp.where(lower, one, two)
                out_refs[3 - flip][at, :, low] = jnp.where(lower, two, one)


def attention_kernel(source_order, grad_order, *refs):
    in_refs, kv_ref, dq_refs, dkv_ref, flat_ref = refs[:4], refs[4], refs[5:9], refs[9], refs[10]
    held = kv_ref.shape[1]
    for at, block in enumerate(source_order):
        flat_ref[block * held : (block + 1) * held, :] = kv_ref[at].astype(F32)
    sources, width = flat_ref.shape[0], flat_ref.shape[1] // 2
    blocks = sources // held
    places = {member: at for at, member in enumerate(grad_order)}
    rows = in_refs[0].shape[1]
    for low in range(0, width, PAIR):
        cols = slice(low, low + PAIR)
        k2 = split_lanes(flat_ref[:, cols].astype(BF16))
        v2 = split_lanes(flat_ref[:, width + low : width + low + PAIR].astype(BF16))
        q = jnp.concatenate([ref[0, :, cols] for ref in in_refs], axis=0)
        do = jnp.concatenate([ref[1, :, cols] for ref in in_refs], axis=0)
        score = (matmul_bt(k2, q) * (SCALE * LOG2E)).reshape(2, sources, 4 * rows)
        dprob = matmul_bt(v2, do).reshape(2, sources, 4 * rows)
        expo = jnp.exp2(score - jnp.max(score, axis=1, keepdims=True))
        probs = expo * (1.0 / jnp.sum(expo, axis=1, keepdims=True))
        p_low = probs.astype(BF16)
        delta = jnp.sum(p_low.astype(F32) * dprob, axis=1, keepdims=True)
        ds_low = (probs * (dprob - delta)).astype(BF16)
        dk = matmul(jnp.concatenate([ds_low[0], ds_low[1]], axis=1), split_lanes(q)) * SCALE
        dv = matmul(jnp.concatenate([p_low[0], p_low[1]], axis=1), split_lanes(do))
        for part in range(2):
            both = join(dk, dv, part)
            first = (low // HD + part) * blocks
            for at in range(blocks):
                dkv_ref[places[first + at]] = both[at * held : (at + 1) * held].astype(BF16)
        dq_t = (matmul(k2.T, ds_low.reshape(2 * sources, 4 * rows)) * SCALE).astype(BF16)
        for at, dq_ref in enumerate(dq_refs):
            dq_ref[:, cols] = dq_t[:, at * rows : (at + 1) * rows].T


def assemble_kernel(own_ref, side_ref, both_ref, core_ref, dq_ref):
    lower, side = lax.axis_index("core") == 0, lax.axis_index("xl")
    for flip, (near_ref, far_ref) in enumerate(((own_ref, core_ref), (side_ref, both_ref))):
        for pair in range(2):
            low = slice(pair * PAIR, (pair + 1) * PAIR)
            near, far = near_ref[:, low].astype(F32), far_ref[:, low].astype(F32)
            one, two = jnp.where(lower, near, far), jnp.where(lower, far, near)
            for x in range(2):
                dq_ref[:, columns(side ^ flip, pair, x)] = join(one, two, x).astype(BF16)


def total_kernel(parts_ref, dk_ref, dv_ref):
    one, two = (sum_parts(parts_ref, core) for core in range(2))
    dk_ref[...] = join(one, two, 0).astype(BF16)
    dv_ref[...] = join(one, two, 1).astype(BF16)


def sum_parts(parts_ref, core):
    terms = [parts_ref[at].astype(F32) for at in range(core, parts_ref.shape[0], 2)]
    while len(terms) > 1:
        terms = [a + b for a, b in zip(terms[::2], terms[1::2])]
    return terms[0]


def call(kernel, out, *args, last=pltpu.VMEM, scratch=(), flops=0, transcendentals=0):
    vmem = pl.BlockSpec(memory_space=pltpu.VMEM)
    size = sum(a.size * a.dtype.itemsize for a in args) + sum(2 * math.prod(s) for s in out)
    return pl.pallas_call(
        kernel,
        out_shape=tuple(jax.ShapeDtypeStruct(s, BF16) for s in out),
        in_specs=[vmem] * len(args),
        out_specs=(vmem,) * (len(out) - 1) + (pl.BlockSpec(memory_space=last),),
        scratch_shapes=scratch,
        compiler_params=pltpu.CompilerParams(vmem_limit_bytes=32 * 1024 * 1024),
        cost_estimate=pl.CostEstimate(flops=flops, bytes_accessed=size, transcendentals=transcendentals),
    )(*args)


def members(orders):
    sizes = [len(order) for order in orders]
    return [int(np.ravel_multi_index(place, sizes)) for place in itertools.product(*orders)]


def trade(own, side, both, core):
    side = lax.ppermute(side, "xl", CORE_SWAP)
    both = lax.ppermute(both, ("xl", "core"), BOTH_SWAP)
    core = lax.ppermute(core, "core", CORE_SWAP)
    return own, side, both, core


def run_attention(source_order, grad_order, *args):
    _, rows, width = args[0].shape
    blocks, held, _ = args[-1].shape
    sources = blocks * held
    pairs = 4 * rows * sources * width // HD
    return call(
        functools.partial(attention_kernel, source_order, grad_order),
        [(rows, width)] * 4 + [(len(grad_order), held, PAIR)],
        *args,
        scratch=[pltpu.VMEM((sources, 2 * width), F32)],
        flops=20 * HD * pairs,
        transcendentals=pairs,
    )


def shards(queries, keys, values, out_grad):
    rows, model = queries.shape
    held = keys.shape[0]
    width = model // 4
    source_order = [(z * 4 + y) * 2 + c for y in (2, 3, 0, 1) for z in (7, 0, 1, 2, 3, 4, 5, 6) for c in range(2)]
    grad_order = members(GRAD_ORDER)
    blocks = len(source_order)
    sources = held * blocks

    (spread,) = call(functools.partial(spread_kernel, source_order), [(blocks, held, 2 * width)], jnp.concatenate([keys, values], axis=0))
    kv = lax.all_to_all(spread, SOURCE_AXES, 0, 0, axis_index_groups=[source_order], tiled=True)
    targets = trade(*call(quarter_kernel, [(2, rows, width)] * 4, queries, out_grad))

    *dq, dkv = run_attention(source_order, grad_order, *targets, kv)
    parts = lax.all_to_all(dkv, GRAD_AXES, 0, 0, axis_index_groups=[grad_order], tiled=True)
    (query_grad,) = call(assemble_kernel, [(rows, model)], *trade(*dq))
    key_grad, value_grad = call(total_kernel, [(held, PAIR), (held, PAIR)], parts)
    return query_grad, key_grad, value_grad


def solution(mesh):
    fine = Mesh(mesh.devices.reshape(2, 2, 2, 8, 4, 2), AXES)
    return jax.shard_map(
        shards,
        mesh=fine,
        in_specs=(P(AXES, None), P(AXES[3:], None), P(AXES[3:], None), P(AXES, None)),
        out_specs=(P(AXES, None), P(AXES[3:], AXES[:3]), P(AXES[3:], AXES[:3])),
        check_vma=False,
    )
```

```python
import functools
import itertools
import math

import jax
import jax.numpy as jnp
import numpy as np
from jax import lax
from jax.experimental import pallas as pl
from jax.experimental.pallas import tpu as pltpu
from jax.sharding import Mesh, PartitionSpec as P

HD = 64
PAIR = 2 * HD
SCALE = HD ** (-0.5)
LOG2E = 1.4426950408889634
BF16 = jnp.bfloat16
F32 = jnp.float32
AXES = ("xh", "xl", "ylo", "z", "yhi", "core")
SOURCE_AXES = ("z", "yhi", "core")
GRAD_AXES = ("xh", "ylo", "z", "yhi", "core")
SOURCE_ORDER = ((7, 0, 1, 2, 3, 4, 5, 6), (2, 3, 0, 1), (0, 1))
GRAD_ORDER = ((1, 0), (0, 1), (5, 6, 7, 0, 1, 2, 3, 4), (0, 1, 2, 3), (0, 1))
CORE_SWAP = [(0, 1), (1, 0)]
BOTH_SWAP = [(0, 3), (1, 2), (2, 1), (3, 0)]


def matmul(a, b):
    return lax.dot_general(a, b, (((1,), (0,)), ((), ())), preferred_element_type=F32)


def matmul_bt(a, b):
    return lax.dot_general(a, b, (((1,), (1,)), ((), ())), preferred_element_type=F32)


def split_lanes(a):
    first = lax.broadcasted_iota(jnp.int32, a.shape, 1) < HD
    zero = jnp.zeros_like(a)
    return jnp.concatenate([jnp.where(first, a, zero), jnp.where(first, zero, a)], axis=0)


def join(a, b, part):
    cols = slice(part * HD, (part + 1) * HD)
    return jnp.concatenate([a[:, cols], b[:, cols]], axis=1)


def columns(side, pair, x):
    return pl.ds(pl.multiple_of((4 * pair + 2 * side + x) * PAIR, PAIR), PAIR)


def core_columns(ref, side, pair):
    a, b = (ref[:, columns(side, pair, x)].astype(F32) for x in range(2))
    return join(a, b, 0).astype(ref.dtype), join(a, b, 1).astype(ref.dtype)


def spread_kernel(order, kv_ref, out_ref):
    side = lax.axis_index("xl")
    held = out_ref.shape[1]
    pieces = []
    for pair in range(2):
        a, b = (kv_ref[:, columns(side, pair, x)].astype(F32) for x in range(2))
        pieces.append([join(a, b, core) for core in range(2)])
    for core in range(2):
        parts = [piece[core][low : low + held] for low in (0, held) for piece in pieces]
        block = jnp.concatenate(parts, axis=1).astype(BF16)
        for at, member in enumerate(order):
            if member % 2 == core:
                out_ref[at] = block


def quarter_kernel(q_ref, do_ref, *out_refs):
    lower, side = lax.axis_index("core") == 0, lax.axis_index("xl")
    for flip in range(2):
        for pair in range(2):
            low = slice(pair * PAIR, (pair + 1) * PAIR)
            for at, ref in enumerate((q_ref, do_ref)):
                one, two = core_columns(ref, side ^ flip, pair)
                out_refs[flip][at, :, low] = jnp.where(lower, one, two)
                out_refs[3 - flip][at, :, low] = jnp.where(lower, two, one)


def attention_kernel(source_order, grad_order, *refs):
    in_refs, kv_ref, dq_refs, dkv_ref, flat_ref = refs[:4], refs[4], refs[5:9], refs[9], refs[10]
    held = kv_ref.shape[1]
    for at, block in enumerate(source_order):
        flat_ref[block * held : (block + 1) * held, :] = kv_ref[at].astype(F32)
    sources, width = flat_ref.shape[0], flat_ref.shape[1] // 2
    blocks = sources // held
    places = {member: at for at, member in enumerate(grad_order)}
    rows = in_refs[0].shape[1]
    for low in range(0, width, PAIR):
        cols = slice(low, low + PAIR)
        k2 = split_lanes(flat_ref[:, cols].astype(BF16))
        v2 = split_lanes(flat_ref[:, width + low : width + low + PAIR].astype(BF16))
        q = jnp.concatenate([ref[0, :, cols] for ref in in_refs], axis=0)
        do = jnp.concatenate([ref[1, :, cols] for ref in in_refs], axis=0)
        score = (matmul_bt(k2, q) * (SCALE * LOG2E)).reshape(2, sources, 4 * rows)
        dprob = matmul_bt(v2, do).reshape(2, sources, 4 * rows)
        expo = jnp.exp2(score - jnp.max(score, axis=1, keepdims=True))
        probs = expo * (1.0 / jnp.sum(expo, axis=1, keepdims=True))
        p_low = probs.astype(BF16)
        delta = jnp.sum(p_low.astype(F32) * dprob, axis=1, keepdims=True)
        ds_low = (probs * (dprob - delta)).astype(BF16)
        dk = matmul(jnp.concatenate([ds_low[0], ds_low[1]], axis=1), split_lanes(q)) * SCALE
        dv = matmul(jnp.concatenate([p_low[0], p_low[1]], axis=1), split_lanes(do))
        for part in range(2):
            both = join(dk, dv, part)
            first = (low // HD + part) * blocks
            for at in range(blocks):
                dkv_ref[places[first + at]] = both[at * held : (at + 1) * held].astype(BF16)
        dq_t = (matmul(k2.T, ds_low.reshape(2 * sources, 4 * rows)) * SCALE).astype(BF16)
        for at, dq_ref in enumerate(dq_refs):
            dq_ref[:, cols] = dq_t[:, at * rows : (at + 1) * rows].T


def assemble_kernel(own_ref, side_ref, both_ref, core_ref, dq_ref):
    lower, side = lax.axis_index("core") == 0, lax.axis_index("xl")
    for flip, (near_ref, far_ref) in enumerate(((own_ref, core_ref), (side_ref, both_ref))):
        for pair in range(2):
            low = slice(pair * PAIR, (pair + 1) * PAIR)
            near, far = near_ref[:, low].astype(F32), far_ref[:, low].astype(F32)
            one, two = jnp.where(lower, near, far), jnp.where(lower, far, near)
            for x in range(2):
                dq_ref[:, columns(side ^ flip, pair, x)] = join(one, two, x).astype(BF16)


def total_kernel(parts_ref, dk_ref, dv_ref):
    one, two = (sum_parts(parts_ref, core) for core in range(2))
    dk_ref[...] = join(one, two, 0).astype(BF16)
    dv_ref[...] = join(one, two, 1).astype(BF16)


def sum_parts(parts_ref, core):
    terms = [parts_ref[at].astype(F32) for at in range(core, parts_ref.shape[0], 2)]
    while len(terms) > 1:
        terms = [a + b for a, b in zip(terms[::2], terms[1::2])]
    return terms[0]


def call(kernel, out, *args, last=pltpu.VMEM, scratch=(), flops=0, transcendentals=0):
    vmem = pl.BlockSpec(memory_space=pltpu.VMEM)
    size = sum(a.size * a.dtype.itemsize for a in args) + sum(2 * math.prod(s) for s in out)
    return pl.pallas_call(
        kernel,
        out_shape=tuple(jax.ShapeDtypeStruct(s, BF16) for s in out),
        in_specs=[vmem] * len(args),
        out_specs=(vmem,) * (len(out) - 1) + (pl.BlockSpec(memory_space=last),),
        scratch_shapes=scratch,
        compiler_params=pltpu.CompilerParams(vmem_limit_bytes=32 * 1024 * 1024),
        cost_estimate=pl.CostEstimate(flops=flops, bytes_accessed=size, transcendentals=transcendentals),
    )(*args)


def members(orders):
    sizes = [len(order) for order in orders]
    return [int(np.ravel_multi_index(place, sizes)) for place in itertools.product(*orders)]


def trade(own, side, both, core):
    side = lax.ppermute(side, "xl", CORE_SWAP)
    both = lax.ppermute(both, ("xl", "core"), BOTH_SWAP)
    core = lax.ppermute(core, "core", CORE_SWAP)
    return own, side, both, core


def run_attention(source_order, grad_order, *args):
    _, rows, width = args[0].shape
    blocks, held, _ = args[-1].shape
    sources = blocks * held
    pairs = 4 * rows * sources * width // HD
    return call(
        functools.partial(attention_kernel, source_order, grad_order),
        [(rows, width)] * 4 + [(len(grad_order), held, PAIR)],
        *args,
        scratch=[pltpu.VMEM((sources, 2 * width), F32)],
        flops=20 * HD * pairs,
        transcendentals=pairs,
    )


def shards(queries, keys, values, out_grad):
    rows, model = queries.shape
    held = keys.shape[0]
    width = model // 4
    source_order = [(z * 4 + y) * 2 + c for y in (2, 3, 0, 1) for z in (6, 7, 0, 1, 2, 3, 4, 5) for c in range(2)]
    grad_order = members(GRAD_ORDER)
    blocks = len(source_order)
    sources = held * blocks

    (spread,) = call(functools.partial(spread_kernel, source_order), [(blocks, held, 2 * width)], jnp.concatenate([keys, values], axis=0))
    kv = lax.all_to_all(spread, SOURCE_AXES, 0, 0, axis_index_groups=[source_order], tiled=True)
    targets = trade(*call(quarter_kernel, [(2, rows, width)] * 4, queries, out_grad))

    *dq, dkv = run_attention(source_order, grad_order, *targets, kv)
    parts = lax.all_to_all(dkv, GRAD_AXES, 0, 0, axis_index_groups=[grad_order], tiled=True)
    (query_grad,) = call(assemble_kernel, [(rows, model)], *trade(*dq))
    key_grad, value_grad = call(total_kernel, [(held, PAIR), (held, PAIR)], parts)
    return query_grad, key_grad, value_grad


def solution(mesh):
    fine = Mesh(mesh.devices.reshape(2, 2, 2, 8, 4, 2), AXES)
    return jax.shard_map(
        shards,
        mesh=fine,
        in_specs=(P(AXES, None), P(AXES[3:], None), P(AXES[3:], None), P(AXES, None)),
        out_specs=(P(AXES, None), P(AXES[3:], AXES[:3]), P(AXES[3:], AXES[:3])),
        check_vma=False,
    )
```

```python
import functools
import itertools
import math

import jax
import jax.numpy as jnp
import numpy as np
from jax import lax
from jax.experimental import pallas as pl
from jax.experimental.pallas import tpu as pltpu
from jax.sharding import Mesh, PartitionSpec as P

HD = 64
PAIR = 2 * HD
SCALE = HD ** (-0.5)
LOG2E = 1.4426950408889634
BF16 = jnp.bfloat16
F32 = jnp.float32
AXES = ("xh", "xl", "ylo", "z", "yhi", "core")
SOURCE_AXES = ("z", "yhi", "core")
GRAD_AXES = ("xh", "ylo", "z", "yhi", "core")
SOURCE_ORDER = ((7, 0, 1, 2, 3, 4, 5, 6), (2, 3, 0, 1), (0, 1))
GRAD_ORDER = ((1, 0), (0, 1), (5, 6, 7, 0, 1, 2, 3, 4), (0, 1, 2, 3), (0, 1))
CORE_SWAP = [(0, 1), (1, 0)]
BOTH_SWAP = [(0, 3), (1, 2), (2, 1), (3, 0)]


def matmul(a, b):
    return lax.dot_general(a, b, (((1,), (0,)), ((), ())), preferred_element_type=F32)


def matmul_bt(a, b):
    return lax.dot_general(a, b, (((1,), (1,)), ((), ())), preferred_element_type=F32)


def split_lanes(a):
    first = lax.broadcasted_iota(jnp.int32, a.shape, 1) < HD
    zero = jnp.zeros_like(a)
    return jnp.concatenate([jnp.where(first, a, zero), jnp.where(first, zero, a)], axis=0)


def join(a, b, part):
    cols = slice(part * HD, (part + 1) * HD)
    return jnp.concatenate([a[:, cols], b[:, cols]], axis=1)


def columns(side, pair, x):
    return pl.ds(pl.multiple_of((4 * pair + 2 * side + x) * PAIR, PAIR), PAIR)


def core_columns(ref, side, pair):
    a, b = (ref[:, columns(side, pair, x)].astype(F32) for x in range(2))
    return join(a, b, 0).astype(ref.dtype), join(a, b, 1).astype(ref.dtype)


def spread_kernel(order, kv_ref, out_ref):
    side = lax.axis_index("xl")
    held = out_ref.shape[1]
    pieces = []
    for pair in range(2):
        a, b = (kv_ref[:, columns(side, pair, x)].astype(F32) for x in range(2))
        pieces.append([join(a, b, core) for core in range(2)])
    for core in range(2):
        parts = [piece[core][low : low + held] for low in (0, held) for piece in pieces]
        block = jnp.concatenate(parts, axis=1).astype(BF16)
        for at, member in enumerate(order):
            if member % 2 == core:
                out_ref[at] = block


def quarter_kernel(q_ref, do_ref, *out_refs):
    lower, side = lax.axis_index("core") == 0, lax.axis_index("xl")
    for flip in range(2):
        for pair in range(2):
            low = slice(pair * PAIR, (pair + 1) * PAIR)
            for at, ref in enumerate((q_ref, do_ref)):
                one, two = core_columns(ref, side ^ flip, pair)
                out_refs[flip][at, :, low] = jnp.where(lower, one, two)
                out_refs[3 - flip][at, :, low] = jnp.where(lower, two, one)


def attention_kernel(source_order, grad_order, *refs):
    in_refs, kv_ref, dq_refs, dkv_ref, flat_ref = refs[:4], refs[4], refs[5:9], refs[9], refs[10]
    held = kv_ref.shape[1]
    for at, block in enumerate(source_order):
        flat_ref[block * held : (block + 1) * held, :] = kv_ref[at].astype(F32)
    sources, width = flat_ref.shape[0], flat_ref.shape[1] // 2
    blocks = sources // held
    places = {member: at for at, member in enumerate(grad_order)}
    rows = in_refs[0].shape[1]
    for low in range(0, width, PAIR):
        cols = slice(low, low + PAIR)
        k2 = split_lanes(flat_ref[:, cols].astype(BF16))
        v2 = split_lanes(flat_ref[:, width + low : width + low + PAIR].astype(BF16))
        q = jnp.concatenate([ref[0, :, cols] for ref in in_refs], axis=0)
        do = jnp.concatenate([ref[1, :, cols] for ref in in_refs], axis=0)
        score = (matmul_bt(k2, q) * (SCALE * LOG2E)).reshape(2, sources, 4 * rows)
        dprob = matmul_bt(v2, do).reshape(2, sources, 4 * rows)
        expo = jnp.exp2(score - jnp.max(score, axis=1, keepdims=True))
        probs = expo * (1.0 / jnp.sum(expo, axis=1, keepdims=True))
        p_low = probs.astype(BF16)
        delta = jnp.sum(p_low.astype(F32) * dprob, axis=1, keepdims=True)
        ds_low = (probs * (dprob - delta)).astype(BF16)
        dk = matmul(jnp.concatenate([ds_low[0], ds_low[1]], axis=1), split_lanes(q)) * SCALE
        dv = matmul(jnp.concatenate([p_low[0], p_low[1]], axis=1), split_lanes(do))
        for part in range(2):
            both = join(dk, dv, part)
            first = (low // HD + part) * blocks
            for at in range(blocks):
                dkv_ref[places[first + at]] = both[at * held : (at + 1) * held].astype(BF16)
        dq_t = (matmul(k2.T, ds_low.reshape(2 * sources, 4 * rows)) * SCALE).astype(BF16)
        for at, dq_ref in enumerate(dq_refs):
            dq_ref[:, cols] = dq_t[:, at * rows : (at + 1) * rows].T


def finish_kernel(own_ref, side_ref, both_ref, core_ref, parts_ref, dq_ref, dk_ref, dv_ref):
    lower, side = lax.axis_index("core") == 0, lax.axis_index("xl")
    for flip, (near_ref, far_ref) in enumerate(((own_ref, core_ref), (side_ref, both_ref))):
        for pair in range(2):
            low = slice(pair * PAIR, (pair + 1) * PAIR)
            near, far = near_ref[:, low].astype(F32), far_ref[:, low].astype(F32)
            one, two = jnp.where(lower, near, far), jnp.where(lower, far, near)
            for x in range(2):
                dq_ref[:, columns(side ^ flip, pair, x)] = join(one, two, x).astype(BF16)
    one, two = (sum_parts(parts_ref, core) for core in range(2))
    dk_ref[...] = join(one, two, 0).astype(BF16)
    dv_ref[...] = join(one, two, 1).astype(BF16)


def sum_parts(parts_ref, core):
    terms = [parts_ref[at].astype(F32) for at in range(core, parts_ref.shape[0], 2)]
    while len(terms) > 1:
        terms = [a + b for a, b in zip(terms[::2], terms[1::2])]
    return terms[0]


def call(kernel, out, *args, last=pltpu.VMEM, scratch=(), flops=0, transcendentals=0):
    vmem = pl.BlockSpec(memory_space=pltpu.VMEM)
    size = sum(a.size * a.dtype.itemsize for a in args) + sum(2 * math.prod(s) for s in out)
    return pl.pallas_call(
        kernel,
        out_shape=tuple(jax.ShapeDtypeStruct(s, BF16) for s in out),
        in_specs=[vmem] * len(args),
        out_specs=(vmem,) * (len(out) - 1) + (pl.BlockSpec(memory_space=last),),
        scratch_shapes=scratch,
        compiler_params=pltpu.CompilerParams(vmem_limit_bytes=32 * 1024 * 1024),
        cost_estimate=pl.CostEstimate(flops=flops, bytes_accessed=size, transcendentals=transcendentals),
    )(*args)


def members(orders):
    sizes = [len(order) for order in orders]
    return [int(np.ravel_multi_index(place, sizes)) for place in itertools.product(*orders)]


def trade(own, side, both, core):
    side = lax.ppermute(side, "xl", CORE_SWAP)
    both = lax.ppermute(both, ("xl", "core"), BOTH_SWAP)
    core = lax.ppermute(core, "core", CORE_SWAP)
    return own, side, both, core


def run_attention(source_order, grad_order, *args):
    _, rows, width = args[0].shape
    blocks, held, _ = args[-1].shape
    sources = blocks * held
    pairs = 4 * rows * sources * width // HD
    return call(
        functools.partial(attention_kernel, source_order, grad_order),
        [(rows, width)] * 4 + [(len(grad_order), held, PAIR)],
        *args,
        scratch=[pltpu.VMEM((sources, 2 * width), F32)],
        flops=20 * HD * pairs,
        transcendentals=pairs,
    )


def shards(queries, keys, values, out_grad):
    rows, model = queries.shape
    held = keys.shape[0]
    width = model // 4
    source_order = [(z * 4 + y) * 2 + c for y in (2, 3, 0, 1) for z in (6, 7, 0, 1, 2, 3, 4, 5) for c in range(2)]
    grad_order = members(GRAD_ORDER)
    blocks = len(source_order)
    sources = held * blocks

    (spread,) = call(functools.partial(spread_kernel, source_order), [(blocks, held, 2 * width)], jnp.concatenate([keys, values], axis=0))
    kv = lax.all_to_all(spread, SOURCE_AXES, 0, 0, axis_index_groups=[source_order], tiled=True)
    targets = trade(*call(quarter_kernel, [(2, rows, width)] * 4, queries, out_grad))

    *dq, dkv = run_attention(source_order, grad_order, *targets, kv)
    parts = lax.all_to_all(dkv, GRAD_AXES, 0, 0, axis_index_groups=[grad_order], tiled=True)
    return call(finish_kernel, [(rows, model), (held, PAIR), (held, PAIR)], *trade(*dq), parts)


def solution(mesh):
    fine = Mesh(mesh.devices.reshape(2, 2, 2, 8, 4, 2), AXES)
    return jax.shard_map(
        shards,
        mesh=fine,
        in_specs=(P(AXES, None), P(AXES[3:], None), P(AXES[3:], None), P(AXES, None)),
        out_specs=(P(AXES, None), P(AXES[3:], AXES[:3]), P(AXES[3:], AXES[:3])),
        check_vma=False,
    )
```
